32 devices in a mesh: tm: 8 (over z, core), lat: 4 (over y, x).
Axes of the slice: x: 2, y: 2, z: 4, core: 2. Of those that a mesh axis runs over, the one named last changes fastest.
Arguments:
- window_snapshots: bfloat16 [8, 64, 32, 128], P('tm', None, 'lat'), may hold values from -6 to 6
- background: bfloat16 [64, 32, 128], P(None, 'lat'), may hold values from -6 to 6
- obs_values: bfloat16 [8, 64, 1024], P('tm', None, 'lat'), may hold values from -6 to 6
- obs_index: int32 [8, 1024], P('tm', 'lat'), may hold values from 0 to 4095, as said below
- input_kernel_weight: bfloat16 [3, 3, 256, 64], replicated, may hold values from -0.25 to 0.25
- hidden_bias_vector: float32 [256], replicated, may hold values from -3 to 3
- output_pointwise_weight: bfloat16 [64, 256], replicated, may hold values from -0.375 to 0.375
Outputs:
- analysis: bfloat16 [8, 64, 32, 128], P('tm', None, 'lat')
The draws below stay inside these ranges and needn't reach their ends.
Inputs may be any that keep to these rules, and one draw needn't show every extreme that they name: `obs_index`: entry [k, j] is a grid column counted latitude by latitude over 128 longitudes; observations s * 256 to (s + 1) * 256 - 1 lie in latitudes s * 8 to (s + 1) * 8 - 1; a column may be observed more than once.
All inputs are finite; a program needn't handle non-finite values.
Results may differ from the reference program's by a relative error of at most 0.015.
Values may be sent and summed in bfloat16 or wider, within the bound.
A program may use at most 64 MiB of HBM per device.

```python
import jax
import jax.numpy as jnp
from jax import lax

C = 64
HID = 256
LAT_DEV = 8
LON = 128
OBS_DEV = 256
ITERS = 2
SUB = 8
LAT = 32
OBS = 1024


def draw_obs_index(key, part):
    strips = OBS // OBS_DEV
    strip_cells = LAT_DEV * LON
    local_cells = jax.random.randint(key, (SUB, strips, OBS_DEV), 0, strip_cells, dtype=jnp.int32)
    local_cells = local_cells.at[:, 0, 0].set(0)
    local_cells = local_cells.at[:, strips - 1, OBS_DEV - 1].set(strip_cells - 1)
    offsets = jnp.arange(strips, dtype=jnp.int32)[None, :, None] * strip_cells
    return (local_cells + offsets).reshape(SUB, OBS).astype(jnp.int32)


def block_levels(own_key, dims, pieces, low, high):
    level, own = 1.0, jax.random.fold_in(own_key, 6)
    for position, parts in pieces:
        heights = jnp.exp(jax.random.uniform(jax.random.fold_in(own, position), (parts,), jnp.float32, low / len(pieces), high / len(pieces)))
        level = level * jnp.repeat(heights, dims[position] // parts).reshape([-1 if axis == position else 1 for axis in range(len(dims))])
    return level


def gaussian(rng, shape, width, limit, shards=(), held_as=jnp.bfloat16):
    level = block_levels(rng, shape, shards, -0.22, 0.18) if shards else 1.0
    values = jax.random.normal(rng, shape, jnp.float32) * width * level
    return jnp.minimum(jnp.maximum(values, -limit), limit).astype(held_as)


def setup_inputs(seed: int = 0) -> dict:
    key_list = jax.random.split(jax.random.key(seed), 8)
    window_snapshots = gaussian(key_list[0], (SUB, C, LAT, LON), 1.0, 6.0, ((0, 8), (2, 4)))
    background = gaussian(key_list[1], (C, LAT, LON), 1.0, 6.0, ((1, 4),))
    obs_values = gaussian(key_list[2], (SUB, C, OBS), 1.0, 6.0, ((0, 8), (2, 4)))
    obs_index = draw_obs_index(jax.random.fold_in(key_list[7], 71), 0)
    input_kernel_weight = gaussian(key_list[4], (3, 3, HID, C), (9 * C) ** -0.5, 0.25)
    hidden_bias_vector = gaussian(key_list[5], (HID,), 0.5, 3.0, (), jnp.float32)
    output_pointwise_weight = gaussian(key_list[6], (C, HID), HID ** -0.5, 0.375)
    return {"window_snapshots": window_snapshots, "background": background, "obs_values": obs_values, "obs_index": obs_index, "input_kernel_weight": input_kernel_weight, "hidden_bias_vector": hidden_bias_vector, "output_pointwise_weight": output_pointwise_weight}


step_size = 0.3


def conv_forward(grid_field, input_kernel_weight):
    height = grid_field.shape[1]
    padded = jnp.pad(grid_field.astype(jnp.float32), ((0, 0), (1, 1), (0, 0)))
    weights = input_kernel_weight.astype(jnp.float32)
    summed = jnp.zeros((input_kernel_weight.shape[2], height, grid_field.shape[2]), jnp.float32)
    for row_step in range(3):
        stripe = padded[:, row_step:row_step + height, :]
        for col_step in range(3):
            moved = jnp.roll(stripe, 1 - col_step, axis=2)
            summed = summed + jnp.einsum("hc,clm->hlm", weights[row_step, col_step], moved, precision=lax.Precision.HIGHEST)
    return summed


def conv_transpose(cotangent, input_kernel_weight):
    height = cotangent.shape[1]
    weights = input_kernel_weight.astype(jnp.float32)
    source = cotangent.astype(jnp.float32)
    summed = jnp.zeros((input_kernel_weight.shape[3], height + 2, cotangent.shape[2]), jnp.float32)
    for row_step in range(3):
        partial_value = jnp.zeros((input_kernel_weight.shape[3], height, cotangent.shape[2]), jnp.float32)
        for col_step in range(3):
            product = jnp.einsum("hc,hlm->clm", weights[row_step, col_step], source, precision=lax.Precision.HIGHEST)
            partial_value = partial_value + jnp.roll(product, col_step - 1, axis=2)
        summed = summed + jnp.pad(partial_value, ((0, 0), (row_step, 2 - row_step), (0, 0)))
    return summed[:, 1:height + 1]


def misfit_map(grid_state, values, column_index):
    channels = grid_state.shape[0]
    flattened = grid_state.reshape(channels, -1)
    misfit = jnp.take(flattened, column_index, axis=1).astype(jnp.float32) - values.astype(jnp.float32)
    spread_out = jnp.zeros(flattened.shape, jnp.float32).at[:, column_index].add(misfit)
    return spread_out.reshape(grid_state.shape)


def reference(window_snapshots, background, obs_values, obs_index, input_kernel_weight, hidden_bias_vector, output_pointwise_weight):
    windows = window_snapshots.shape[0]
    weights_out = output_pointwise_weight.astype(jnp.float32)
    for repeat in range(ITERS):
        def couple(paired):
            earlier_snapshot = paired[0]
            current_snapshot = paired[1]
            before = conv_forward(earlier_snapshot, input_kernel_weight) + hidden_bias_vector[:, None, None]
            active = jnp.tanh(before).astype(jnp.bfloat16)
            latent_activation_layer = jnp.einsum("ch,hlm->clm", weights_out, active.astype(jnp.float32), precision=lax.Precision.HIGHEST)
            surrogate_projection = (earlier_snapshot.astype(jnp.float32) + latent_activation_layer).astype(jnp.bfloat16)
            dynamics_mismatch = (current_snapshot.astype(jnp.float32) - surrogate_projection.astype(jnp.float32)).astype(jnp.bfloat16)
            projected = jnp.einsum("ch,clm->hlm", weights_out, dynamics_mismatch.astype(jnp.float32), precision=lax.Precision.HIGHEST)
            squashed = active.astype(jnp.float32)
            cotangent = ((1.0 - squashed * squashed) * projected).astype(jnp.bfloat16)
            pulled = (dynamics_mismatch.astype(jnp.float32) + conv_transpose(cotangent, input_kernel_weight)).astype(jnp.bfloat16)
            return dynamics_mismatch, pulled

        later_resid, pulled = lax.map(couple, (window_snapshots[:windows - 1], window_snapshots[1:]))
        first_resid = (window_snapshots[0].astype(jnp.float32) - background.astype(jnp.float32)).astype(jnp.bfloat16)
        dynamics_mismatch = jnp.concatenate([first_resid[None], later_resid], axis=0)
        adjoint = jnp.concatenate([pulled, jnp.zeros_like(window_snapshots[:1])], axis=0)
        innovation = lax.map(lambda paired: misfit_map(paired[0], paired[1], paired[2]), (window_snapshots, obs_values, obs_index))
        gradient = dynamics_mismatch.astype(jnp.float32) - adjoint.astype(jnp.float32) + innovation
        window_snapshots = (window_snapshots.astype(jnp.float32) - step_size * gradient).astype(jnp.bfloat16)
    return window_snapshots
```

```python
import functools

import jax
import jax.numpy as jnp
from jax import lax
from jax.experimental import pallas as pl
from jax.experimental.pallas import tpu as pltpu
from jax.sharding import PartitionSpec as P

ITERS = 2
step_size = 0.3
BF = jnp.bfloat16
F32 = jnp.float32
MESH = pl.DeviceIdType.MESH

TO_LOW, TO_HIGH, TO_PREV, TO_PREV_LOW, TO_PREV_HIGH, FC_MID, FC_LOW, FC_HIGH = range(8)
KINDS = 8


def kernel(
    steps, sub, strips,
    x_hbm, bg_hbm, obs_hbm, idx_hbm, w_hbm, b_hbm, p_hbm,
    out_ref,
    x_in, bg_in, obs_in, idx_in, w_in, b_in, p_in,
    xm, xn, fc, fcin, x3, act, cot, res, part, wf, wt, pt, bias, bgr, osum, ocnt,
    in_sem, send_sem, recv_sem,
):
    t = lax.axis_index("tm")
    l = lax.axis_index("lat")
    chans, height, lon = x_in.shape
    hid = p_in.shape[1]
    has_prev, has_next = t > 0, t < sub - 1
    has_low, has_high = l > 0, l < strips - 1
    t_prev, t_next = lax.rem(t + sub - 1, sub), lax.rem(t + 1, sub)
    l_low, l_high = lax.rem(l + strips - 1, strips), lax.rem(l + 1, strips)
    both = jnp.logical_and

    loads = [
        pltpu.make_async_copy(src, dst, in_sem.at[n])
        for n, (src, dst) in enumerate(
            [(x_hbm, x_in), (w_hbm, w_in), (p_hbm, p_in), (b_hbm, b_in),
             (obs_hbm, obs_in), (idx_hbm, idx_in), (bg_hbm, bg_in)]
        )
    ]
    barrier = pltpu.get_barrier_semaphore()

    def greet(ok, tt, ll):
        @pl.when(ok)
        def _():
            pl.semaphore_signal(barrier, inc=1, device_id=(tt, ll), device_id_type=MESH)

    greet(has_low, t, l_low)
    greet(has_high, t, l_high)
    greet(has_next, t_next, l)
    greet(both(has_next, has_low), t_next, l_low)
    greet(both(has_next, has_high), t_next, l_high)
    greet(has_prev, t_prev, l)
    for load in loads:
        load.start()

    def copies(it):
        own = xm.at[it]
        table = {
            TO_LOW: (own.at[pl.ds(2, 2)], own.at[pl.ds(height + 2, 2)], t, l_low, has_low, has_high),
            TO_HIGH: (own.at[pl.ds(height, 2)], own.at[pl.ds(0, 2)], t, l_high, has_high, has_low),
            TO_PREV: (own.at[pl.ds(2, height)], xn.at[it, pl.ds(1, height)], t_prev, l, has_prev, has_next),
            TO_PREV_LOW: (own.at[pl.ds(2, 1)], xn.at[it, pl.ds(height + 1, 1)], t_prev, l_low,
                          both(has_prev, has_low), both(has_next, has_high)),
            TO_PREV_HIGH: (own.at[pl.ds(height + 1, 1)], xn.at[it, pl.ds(0, 1)], t_prev, l_high,
                           both(has_prev, has_high), both(has_next, has_low)),
            FC_MID: (fc.at[it, pl.ds(2, height - 2)], fcin.at[it, pl.ds(1, height - 2)], t_next, l, has_next, has_prev),
            FC_LOW: (fc.at[it, pl.ds(1, 1)], fcin.at[it, pl.ds(0, 1)], t_next, l, has_next, has_prev),
            FC_HIGH: (fc.at[it, pl.ds(height, 1)], fcin.at[it, pl.ds(height - 1, 1)], t_next, l, has_next, has_prev),
        }
        made = {}
        for kind, (src, dst, tt, ll, sends, receives) in table.items():
            made[kind] = (
                pltpu.make_async_remote_copy(
                    src_ref=src, dst_ref=dst,
                    send_sem=send_sem.at[it, kind], recv_sem=recv_sem.at[it, kind],
                    device_id=(tt, ll), device_id_type=MESH,
                ),
                sends, receives,
            )
        return made

    moves = [copies(it) for it in range(steps)]

    def start(it, kind):
        copy, sends, _ = moves[it][kind]
        pl.when(sends)(lambda: copy.start())

    def arrive(it, kind):
        copy, _, receives = moves[it][kind]
        pl.when(receives)(lambda: copy.wait_recv())

    def left(it, kind):
        copy, sends, _ = moves[it][kind]
        pl.when(sends)(lambda: copy.wait_send())

    def send_state(it):
        for kind in (TO_LOW, TO_HIGH, TO_PREV_LOW, TO_PREV_HIGH, TO_PREV):
            start(it, kind)

    loads[0].wait()
    xm[0, 2 : height + 2] = jnp.swapaxes(x_in[...].astype(F32), 0, 1).astype(BF)
    zero2 = jnp.zeros((2, chans, lon), BF)
    for it in range(steps):
        @pl.when(jnp.logical_not(has_low))
        def _():
            xm[it, 0:2] = zero2
            xn[it, 0:1] = zero2[:1]

        @pl.when(jnp.logical_not(has_high))
        def _():
            xm[it, height + 2 : height + 4] = zero2
            xn[it, height + 1 : height + 2] = zero2[:1]

    one = lambda flag: flag.astype(jnp.int32)
    expected = (
        one(has_low) + one(has_high) + one(has_prev) + one(both(has_prev, has_low))
        + one(both(has_prev, has_high)) + one(has_next)
    )
    pl.semaphore_wait(barrier, expected)
    send_state(0)

    loads[1].wait()
    for a in range(3):
        strip = jnp.concatenate([w_in[a, b] for b in range(3)], axis=1)
        wf[:, a * 3 * chans : (a + 1) * 3 * chans] = strip
        wt[:, a * hid : (a + 1) * hid] = strip.astype(F32).T.astype(BF)
    loads[2].wait()
    pt[...] = p_in[...].astype(F32).T.astype(BF)
    loads[3].wait()
    bias[...] = jnp.broadcast_to(b_in[...], (lon, hid)).T
    loads[4].wait()
    loads[5].wait()
    loads[6].wait()
    obs_n = obs_in.shape[1]
    obs1 = jnp.concatenate([obs_in[...], jnp.ones((16, obs_n), BF)], axis=0)
    local = idx_in[...] - l * (height * lon)
    for r in range(height):
        cells = lax.broadcasted_iota(jnp.int32, (lon, obs_n), 0) + r * lon
        hot = jnp.where(cells == local, 1.0, 0.0).astype(BF)
        both_sums = lax.dot_general(obs1, hot, (((1,), (1,)), ((), ())), preferred_element_type=F32)
        osum[r] = both_sums[:chans]
        ocnt[r] = both_sums[chans : chans + 8]

    @pl.when(jnp.logical_not(has_prev))
    def _():
        bgr[...] = jnp.swapaxes(bg_in[...].astype(F32), 0, 1).astype(BF)

    def fill(it, row):
        v = xm[it, row].astype(F32)
        x3[row, 0:chans] = pltpu.roll(v, 1, 1).astype(BF)
        x3[row, chans : 2 * chans] = xm[it, row]
        x3[row, 2 * chans : 3 * chans] = pltpu.roll(v, lon - 1, 1).astype(BF)

    def forward(it, n):
        rhs = jnp.concatenate(
            [jnp.concatenate([x3[n + a], x3[n + 1 + a]], axis=1) for a in range(3)], axis=0
        )
        before = jnp.dot(wf[...], rhs, preferred_element_type=F32)
        b2 = bias[...]
        active = jnp.tanh(before + jnp.concatenate([b2, b2], axis=1)).astype(BF)
        act[n] = active[:, :lon]
        act[n + 1] = active[:, lon:]
        z = jnp.dot(p_in[...], active, preferred_element_type=F32)
        fc[it, n] = (xm[it, n + 1].astype(F32) + z[:, :lon]).astype(BF)
        fc[it, n + 1] = (xm[it, n + 2].astype(F32) + z[:, lon:]).astype(BF)

    def backward(it, n):
        pair = []
        for r in (n, n + 1):
            mis = (xn[it, r].astype(F32) - fc[it, r].astype(F32)).astype(BF)
            if r == 0:
                mis = jnp.where(has_low, mis, jnp.zeros_like(mis))
            if r == height + 1:
                mis = jnp.where(has_high, mis, jnp.zeros_like(mis))
            res[r] = mis
            pair.append(mis)
        projected = jnp.dot(pt[...], jnp.concatenate(pair, axis=1), preferred_element_type=F32)
        for k, r in enumerate((n, n + 1)):
            a = act[r].astype(F32)
            cot[r] = ((1.0 - a * a) * projected[:, k * lon : (k + 1) * lon]).astype(BF)

    def innovation(it, i):
        x = xm[it, i + 2].astype(F32)
        n = ocnt[i]
        many = jnp.concatenate([n] * (chans // 8), axis=0)
        return x * many - osum[i]

    def spread(it, i):
        rhs = jnp.concatenate(
            [jnp.concatenate([cot[i + 2 - a], cot[i + 3 - a]], axis=1) for a in range(3)], axis=0
        )
        g = jnp.dot(wt[...], rhs, preferred_element_type=F32)
        for k in range(2):
            piece = g[:, k * lon : (k + 1) * lon]
            total = (
                pltpu.roll(piece[:chans], lon - 1, 1)
                + piece[chans : 2 * chans]
                + pltpu.roll(piece[2 * chans :], 1, 1)
            )
            adjoint = (res[i + k + 1].astype(F32) + total).astype(BF).astype(F32)
            part[i + k] = innovation(it, i + k) - adjoint

    for it in range(steps):
        @pl.when(has_next)
        def _():
            for row in range(2, height + 2):
                fill(it, row)
            for n in range(2, height, 2):
                forward(it, n)
        start(it, FC_MID)
        arrive(it, TO_LOW)
        arrive(it, TO_HIGH)

        @pl.when(has_next)
        def _():
            for row in (0, 1, height + 2, height + 3):
                fill(it, row)
            forward(it, 0)
            forward(it, height)
        start(it, FC_LOW)
        start(it, FC_HIGH)
        arrive(it, TO_PREV)
        arrive(it, TO_PREV_LOW)
        arrive(it, TO_PREV_HIGH)

        @pl.when(has_next)
        def _():
            for n in range(0, height + 2, 2):
                backward(it, n)
            for i in range(0, height, 2):
                spread(it, i)

        @pl.when(jnp.logical_not(has_next))
        def _():
            for i in range(height):
                part[i] = innovation(it, i)

        for kind in (FC_MID, FC_LOW, FC_HIGH):
            arrive(it, kind)

        @pl.when(jnp.logical_not(has_prev))
        def _():
            fcin[it] = bgr[...]

        for i in range(height):
            x = xm[it, i + 2].astype(F32)
            mis = (x - fcin[it, i].astype(F32)).astype(BF).astype(F32)
            new = (x - step_size * (mis + part[i])).astype(BF)
            if it + 1 < steps:
                xm[it + 1, i + 2] = new
            else:
                out_ref[i] = new
        if it + 1 < steps:
            send_state(it + 1)

    for it in range(steps):
        for kind in range(KINDS):
            left(it, kind)


def on_device(
    mesh_shape, window_snapshots, background, obs_values, obs_index,
    input_kernel_weight, hidden_bias_vector, output_pointwise_weight,
):
    _, chans, height, lon = window_snapshots.shape
    hid = output_pointwise_weight.shape[1]
    obs_n = obs_values.shape[2]
    vmem = pltpu.VMEM
    anywhere = pl.BlockSpec(memory_space=pl.ANY)
    rows = pl.pallas_call(
        functools.partial(kernel, ITERS, mesh_shape["tm"], mesh_shape["lat"]),
        out_shape=jax.ShapeDtypeStruct((height, chans, lon), BF),
        in_specs=[anywhere] * 7,
        out_specs=pl.BlockSpec(memory_space=pltpu.VMEM),
        scratch_shapes=[
            vmem((chans, height, lon), BF),
            vmem((chans, height, lon), BF),
            vmem((chans, obs_n), BF),
            vmem((1, obs_n), jnp.int32),
            vmem(input_kernel_weight.shape, BF),
            vmem((1, hid), F32),
            vmem((chans, hid), BF),
            vmem((ITERS, height + 4, chans, lon), BF),
            vmem((ITERS, height + 2, chans, lon), BF),
            vmem((ITERS, height + 2, chans, lon), BF),
            vmem((ITERS, height, chans, lon), BF),
            vmem((height + 4, 3 * chans, lon), BF),
            vmem((height + 2, hid, lon), BF),
            vmem((height + 2, hid, lon), BF),
            vmem((height + 2, chans, lon), BF),
            vmem((height, chans, lon), F32),
            vmem((hid, 9 * chans), BF),
            vmem((3 * chans, 3 * hid), BF),
            vmem((hid, chans), BF),
            vmem((hid, lon), F32),
            vmem((height, chans, lon), BF),
            vmem((height, chans, lon), F32),
            vmem((height, 8, lon), F32),
            pltpu.SemaphoreType.DMA((7,)),
            pltpu.SemaphoreType.DMA((ITERS, KINDS)),
            pltpu.SemaphoreType.DMA((ITERS, KINDS)),
        ],
        compiler_params=pltpu.CompilerParams(
            collective_id=0, has_side_effects=True, vmem_limit_bytes=32 * 1024 * 1024
        ),
    )(
        window_snapshots[0], background, obs_values[0], obs_index,
        input_kernel_weight, hidden_bias_vector[None], output_pointwise_weight,
    )
    return jnp.swapaxes(rows, 0, 1)[None]


def solution(mesh):
    placed = (
        P("tm", None, "lat", None),
        P(None, "lat", None),
        P("tm", None, "lat"),
        P("tm", "lat"),
        P(),
        P(),
        P(),
    )
    return jax.shard_map(
        functools.partial(on_device, dict(mesh.shape)),
        mesh=mesh, in_specs=placed, out_specs=P("tm", None, "lat", None), check_vma=False,
    )
```

```python
import functools

import jax
import jax.numpy as jnp
from jax import lax
from jax.experimental import pallas as pl
from jax.experimental.pallas import tpu as pltpu
from jax.sharding import PartitionSpec as P

ITERS = 2
step_size = 0.3
BF = jnp.bfloat16
F32 = jnp.float32
MESH = pl.DeviceIdType.MESH

TO_LOW, TO_HIGH, TO_PREV, TO_PREV_LOW, TO_PREV_HIGH, FC_MID, FC_LOW, FC_HIGH = range(8)
KINDS = 8


def kernel(
    steps, sub, strips,
    x_hbm, bg_hbm, obs_hbm, idx_hbm, w_hbm, b_hbm, p_hbm,
    out_ref,
    x_in, bg_in, obs_in, idx_in, w_in, b_in, p_in,
    xm, xn, fc, fcin, x3, act, cot, res, part, wf, wt, pt, bias, bgr, osum, ocnt,
    in_sem, send_sem, recv_sem,
):
    t = lax.axis_index("tm")
    l = lax.axis_index("lat")
    chans, height, lon = x_in.shape
    hid = p_in.shape[1]
    has_prev, has_next = t > 0, t < sub - 1
    has_low, has_high = l > 0, l < strips - 1
    t_prev, t_next = lax.rem(t + sub - 1, sub), lax.rem(t + 1, sub)
    l_low, l_high = lax.rem(l + strips - 1, strips), lax.rem(l + 1, strips)
    both = jnp.logical_and

    loads = [
        pltpu.make_async_copy(src, dst, in_sem.at[n])
        for n, (src, dst) in enumerate(
            [(x_hbm, x_in), (w_hbm, w_in), (p_hbm, p_in), (b_hbm, b_in),
             (obs_hbm, obs_in), (idx_hbm, idx_in), (bg_hbm, bg_in)]
        )
    ]
    barrier = pltpu.get_barrier_semaphore()

    def greet(ok, tt, ll):
        @pl.when(ok)
        def _():
            pl.semaphore_signal(barrier, inc=1, device_id=(tt, ll), device_id_type=MESH)

    greet(has_low, t, l_low)
    greet(has_high, t, l_high)
    greet(has_next, t_next, l)
    greet(both(has_next, has_low), t_next, l_low)
    greet(both(has_next, has_high), t_next, l_high)
    greet(has_prev, t_prev, l)
    for load in loads:
        load.start()

    def copies(it):
        own = xm.at[it]
        table = {
            TO_LOW: (own.at[pl.ds(2, 2)], own.at[pl.ds(height + 2, 2)], t, l_low, has_low, has_high),
            TO_HIGH: (own.at[pl.ds(height, 2)], own.at[pl.ds(0, 2)], t, l_high, has_high, has_low),
            TO_PREV: (own.at[pl.ds(2, height)], xn.at[it, pl.ds(1, height)], t_prev, l, has_prev, has_next),
            TO_PREV_LOW: (own.at[pl.ds(2, 1)], xn.at[it, pl.ds(height + 1, 1)], t_prev, l_low,
                          both(has_prev, has_low), both(has_next, has_high)),
            TO_PREV_HIGH: (own.at[pl.ds(height + 1, 1)], xn.at[it, pl.ds(0, 1)], t_prev, l_high,
                           both(has_prev, has_high), both(has_next, has_low)),
            FC_MID: (fc.at[it, pl.ds(2, height - 2)], fcin.at[it, pl.ds(1, height - 2)], t_next, l, has_next, has_prev),
            FC_LOW: (fc.at[it, pl.ds(1, 1)], fcin.at[it, pl.ds(0, 1)], t_next, l, has_next, has_prev),
            FC_HIGH: (fc.at[it, pl.ds(height, 1)], fcin.at[it, pl.ds(height - 1, 1)], t_next, l, has_next, has_prev),
        }
        made = {}
        for kind, (src, dst, tt, ll, sends, receives) in table.items():
            made[kind] = (
                pltpu.make_async_remote_copy(
                    src_ref=src, dst_ref=dst,
                    send_sem=send_sem.at[it, kind], recv_sem=recv_sem.at[it, kind],
                    device_id=(tt, ll), device_id_type=MESH,
                ),
                sends, receives,
            )
        return made

    moves = [copies(it) for it in range(steps)]

    def start(it, kind):
        copy, sends, _ = moves[it][kind]
        pl.when(sends)(lambda: copy.start())

    def arrive(it, kind):
        copy, _, receives = moves[it][kind]
        pl.when(receives)(lambda: copy.wait_recv())

    def left(it, kind):
        copy, sends, _ = moves[it][kind]
        pl.when(sends)(lambda: copy.wait_send())

    def send_state(it):
        for kind in (TO_LOW, TO_HIGH, TO_PREV_LOW, TO_PREV_HIGH, TO_PREV):
            start(it, kind)

    loads[0].wait()
    xm[0, 2 : height + 2] = jnp.swapaxes(x_in[...].astype(F32), 0, 1).astype(BF)
    zero2 = jnp.zeros((2, chans, lon), BF)
    for it in range(steps):
        @pl.when(jnp.logical_not(has_low))
        def _():
            xm[it, 0:2] = zero2
            xn[it, 0:1] = zero2[:1]

        @pl.when(jnp.logical_not(has_high))
        def _():
            xm[it, height + 2 : height + 4] = zero2
            xn[it, height + 1 : height + 2] = zero2[:1]

    one = lambda flag: flag.astype(jnp.int32)
    expected = (
        one(has_low) + one(has_high) + one(has_prev) + one(both(has_prev, has_low))
        + one(both(has_prev, has_high)) + one(has_next)
    )
    pl.semaphore_wait(barrier, expected)
    send_state(0)

    loads[1].wait()
    for a in range(3):
        strip = jnp.concatenate([w_in[a, b] for b in range(3)], axis=0)
        wt[:, a * hid : (a + 1) * hid] = strip
        wf[:, a * 3 * chans : (a + 1) * 3 * chans] = strip.astype(F32).T.astype(BF)
    loads[2].wait()
    pt[...] = p_in[...].astype(F32).T.astype(BF)
    loads[3].wait()
    bias[...] = jnp.broadcast_to(b_in[...], (lon, hid)).T
    loads[4].wait()
    loads[5].wait()
    loads[6].wait()
    obs_n = obs_in.shape[1]
    obs1 = jnp.concatenate([obs_in[...], jnp.ones((16, obs_n), BF)], axis=0)
    local = idx_in[...] - l * (height * lon)
    for r in range(height):
        cells = lax.broadcasted_iota(jnp.int32, (lon, obs_n), 0) + r * lon
        hot = jnp.where(cells == local, 1.0, 0.0).astype(BF)
        both_sums = lax.dot_general(obs1, hot, (((1,), (1,)), ((), ())), preferred_element_type=F32)
        osum[r] = both_sums[:chans]
        ocnt[r] = both_sums[chans : chans + 8]

    @pl.when(jnp.logical_not(has_prev))
    def _():
        bgr[...] = jnp.swapaxes(bg_in[...].astype(F32), 0, 1).astype(BF)

    def fill(source, target):
        v = source[...].astype(F32)
        target[0:chans] = pltpu.roll(v, 1, 1).astype(BF)
        target[chans : 2 * chans] = source[...]
        target[2 * chans : 3 * chans] = pltpu.roll(v, lon - 1, 1).astype(BF)

    def hidden(operand, rows):
        rhs = jnp.concatenate(
            [jnp.concatenate([operand[r + a] for r in rows], axis=1) for a in range(3)], axis=0
        )
        before = jnp.dot(wf[...], rhs, preferred_element_type=F32)
        return jnp.tanh(before + jnp.concatenate([bias[...]] * len(rows), axis=1)).astype(BF)

    def forward(it, rows):
        active = hidden(x3, rows)
        z = jnp.dot(p_in[...], active, preferred_element_type=F32)
        for k, r in enumerate(rows):
            act[r] = active[:, k * lon : (k + 1) * lon]
            fc[it, r] = (xm[it, r + 1].astype(F32) + z[:, k * lon : (k + 1) * lon]).astype(BF)

    def backward(it, rows):
        parts = []
        for r in rows:
            mis = (xn[it, r].astype(F32) - fc[it, r].astype(F32)).astype(BF)
            if r == 0:
                mis = jnp.where(has_low, mis, jnp.zeros_like(mis))
            if r == height + 1:
                mis = jnp.where(has_high, mis, jnp.zeros_like(mis))
            res[r] = mis
            parts.append(mis)
        projected = jnp.dot(pt[...], jnp.concatenate(parts, axis=1), preferred_element_type=F32)
        for k, r in enumerate(rows):
            a = act[r].astype(F32)
            cot[r] = ((1.0 - a * a) * projected[:, k * lon : (k + 1) * lon]).astype(BF)

    def innovation(it, i):
        x = xm[it, i + 2].astype(F32)
        n = ocnt[i]
        many = jnp.concatenate([n] * (chans // 8), axis=0)
        return x * many - osum[i]

    def spread(it, rows):
        rhs = jnp.concatenate(
            [jnp.concatenate([cot[i + 2 - a] for i in rows], axis=1) for a in range(3)], axis=0
        )
        g = jnp.dot(wt[...], rhs, preferred_element_type=F32)
        for k, i in enumerate(rows):
            piece = g[:, k * lon : (k + 1) * lon]
            total = (
                pltpu.roll(piece[:chans], lon - 1, 1)
                + piece[chans : 2 * chans]
                + pltpu.roll(piece[2 * chans :], 1, 1)
            )
            adjoint = (res[i + 1].astype(F32) + total).astype(BF).astype(F32)
            part[i] = innovation(it, i) - adjoint

    for it in range(steps):
        @pl.when(has_next)
        def _():
            for row in range(2, height + 2):
                fill(xm.at[it, row], x3.at[row])
            for rows in [tuple(range(2, height))]:
                forward(it, rows)
        start(it, FC_MID)
        arrive(it, TO_LOW)
        arrive(it, TO_HIGH)

        @pl.when(has_next)
        def _():
            for row in (0, 1, height + 2, height + 3):
                fill(xm.at[it, row], x3.at[row])
            forward(it, (0, 1, height, height + 1))
        start(it, FC_LOW)
        start(it, FC_HIGH)
        arrive(it, TO_PREV)
        arrive(it, TO_PREV_LOW)
        arrive(it, TO_PREV_HIGH)

        @pl.when(has_next)
        def _():
            for rows in [tuple(range(height + 2))]:
                backward(it, rows)
            for rows in [tuple(range(height))]:
                spread(it, rows)

        @pl.when(jnp.logical_not(has_next))
        def _():
            for i in range(height):
                part[i] = innovation(it, i)

        for kind in (FC_MID, FC_LOW, FC_HIGH):
            arrive(it, kind)

        @pl.when(jnp.logical_not(has_prev))
        def _():
            fcin[it] = bgr[...]

        for i in range(height):
            x = xm[it, i + 2].astype(F32)
            mis = (x - fcin[it, i].astype(F32)).astype(BF).astype(F32)
            new = (x - step_size * (mis + part[i])).astype(BF)
            if it + 1 < steps:
                xm[it + 1, i + 2] = new
            else:
                out_ref[i] = new
        if it + 1 < steps:
            send_state(it + 1)

    for it in range(steps):
        for kind in range(KINDS):
            left(it, kind)


def on_device(
    mesh_shape, window_snapshots, background, obs_values, obs_index,
    input_kernel_weight, hidden_bias_vector, output_pointwise_weight,
):
    _, chans, height, lon = window_snapshots.shape
    hid = output_pointwise_weight.shape[1]
    obs_n = obs_values.shape[2]
    vmem = pltpu.VMEM
    anywhere = pl.BlockSpec(memory_space=pltpu.HBM)
    rows = pl.pallas_call(
        functools.partial(kernel, ITERS, mesh_shape["tm"], mesh_shape["lat"]),
        out_shape=pltpu.VMEM((height, chans, lon), BF),
        in_specs=[anywhere] * 7,
        out_specs=pl.BlockSpec(memory_space=pltpu.VMEM),
        scratch_shapes=[
            vmem((chans, height, lon), BF),
            vmem((chans, height, lon), BF),
            vmem((chans, obs_n), BF),
            vmem((1, obs_n), jnp.int32),
            vmem((3, 3, chans, hid), BF),
            vmem((1, hid), F32),
            vmem((chans, hid), BF),
            vmem((ITERS, height + 4, chans, lon), BF),
            vmem((ITERS, height + 2, chans, lon), BF),
            vmem((ITERS, height + 2, chans, lon), BF),
            vmem((ITERS, height, chans, lon), BF),
            vmem((height + 4, 3 * chans, lon), BF),
            vmem((height + 2, hid, lon), BF),
            vmem((height + 2, hid, lon), BF),
            vmem((height + 2, chans, lon), BF),
            vmem((height, chans, lon), F32),
            vmem((hid, 9 * chans), BF),
            vmem((3 * chans, 3 * hid), BF),
            vmem((hid, chans), BF),
            vmem((hid, lon), F32),
            vmem((height, chans, lon), BF),
            vmem((height, chans, lon), F32),
            vmem((height, 8, lon), F32),
            pltpu.SemaphoreType.DMA((7,)),
            pltpu.SemaphoreType.DMA((ITERS, KINDS)),
            pltpu.SemaphoreType.DMA((ITERS, KINDS)),
        ],
        compiler_params=pltpu.CompilerParams(
            collective_id=0, has_side_effects=True, vmem_limit_bytes=60 * 1024 * 1024
        ),
    )(
        window_snapshots[0], background, obs_values[0], obs_index,
        jnp.swapaxes(input_kernel_weight, 2, 3), hidden_bias_vector[None], output_pointwise_weight,
    )
    return jnp.swapaxes(rows, 0, 1)[None]


def solution(mesh):
    placed = (
        P("tm", None, "lat", None),
        P(None, "lat", None),
        P("tm", None, "lat"),
        P("tm", "lat"),
        P(),
        P(),
        P(),
    )
    return jax.shard_map(
        functools.partial(on_device, dict(mesh.shape)),
        mesh=mesh, in_specs=placed, out_specs=P("tm", None, "lat", None), check_vma=False,
    )
```
